512 devices in a mesh: frame: 16 (over z), chan: 32 (over x, y, core).
Axes of the slice: x: 4, y: 4, z: 16, core: 2. Of those that a mesh axis runs over, the one named last changes fastest.
Arguments:
- features: bfloat16 [38912, 3072], P('frame', 'chan'), may hold values from -6 to 6
- w_value: bfloat16 [3072, 2048], P(None, 'chan'), may hold values from -0.109375 to 0.109375
- w_out: bfloat16 [2048, 3072], P(None, 'chan'), may hold values from -0.125 to 0.125
- maps: bfloat16 [16, 16, 4, 128, 128], P(None, 'frame'), may hold values from 0.0009994507 to 0.099609375
- lists: int32 [16, 16, 4], replicated, may hold values from 0 to 303, as said below
Outputs:
- mixed: bfloat16 [2048, 3072], P('frame', 'chan')
The draws below stay inside these ranges and needn't reach their ends.
Inputs may be any that keep to these rules, and one draw needn't show every extreme that they name: `lists`: the 4 blocks of one list lie on 4 different indices of frame: their numbers integer-divided by 19 differ.
All inputs are finite; a program needn't handle non-finite values.
Results may differ from the reference program's by a relative error of at most 0.0057.
Values may be sent and summed in bfloat16 or wider, within the bound.
No kernel may reach another device: no remote copies, remote signals or barrier semaphores. Data moves between devices by JAX's collectives and lax.ppermute only.
A program may use at most 64 MiB of HBM per device.

```python
import math
import jax
import jax.numpy as jnp
from jax import lax

D = 3072
HEADS = 16
HEAD_DIM = 128
BLK = 128
LIST = 4
KV_DEV = 2432
ATT = 2048
KTOKENS = 38912
KBLOCKS = 304
QBLOCKS = 16
N_FRAME = 16


def draw_lists(key, part):
    base = jax.random.fold_in(key, 7)
    key_pop, key_score, key_inner = jax.random.split(base, 3)
    per_frame = KV_DEV // BLK
    popular = jax.random.randint(key_pop, (N_FRAME,), 0, 1024, dtype=jnp.int32)
    score = jax.random.randint(key_score, (HEADS, QBLOCKS, N_FRAME), 0, 1024, dtype=jnp.int32) + popular
    score = score.at[0, 0, N_FRAME - 1].add(4096)
    score = score.at[1, 0, 0].add(4096)
    distinct = score * N_FRAME + jnp.arange(N_FRAME, dtype=jnp.int32)
    picked = lax.top_k(distinct, LIST)[1].astype(jnp.int32)
    inner = jax.random.randint(key_inner, (HEADS, QBLOCKS, LIST), 0, per_frame, dtype=jnp.int32)
    inner = inner.at[0, 0, :].set(per_frame - 1)
    inner = inner.at[1, 0, :].set(0)
    return (picked * per_frame + inner).astype(jnp.int32)


def block_scale(key, extent, shards, low, top_value):
    loudness = 1.0
    for axis_at, blocks in shards:
        draws = jax.random.uniform(jax.random.fold_in(jax.random.fold_in(key, 6), axis_at), (blocks,), jnp.float32, low / len(shards), top_value / len(shards))
        loudness = loudness * jnp.repeat(jnp.exp(draws), extent[axis_at] // blocks).reshape((-1,) + (1,) * (len(extent) - 1 - axis_at))
    return loudness


def normal_values(key, dims, deviation, limit, cuts=(), kind=jnp.bfloat16):
    array = jax.random.normal(key, dims, jnp.float32) * deviation
    if len(cuts) > 0:
        array = block_scale(key, dims, cuts, -0.22, 0.18) * array
    return jnp.clip(array, min=-limit, max=limit).astype(kind)


def setup_inputs(seed: int = 0) -> dict:
    seeds = jax.random.split(jax.random.key(seed), 6)
    return {
        "features": normal_values(seeds[0], (KTOKENS, D), 1.0, 6.0, ((0, 16), (1, 32))),
        "w_value": normal_values(seeds[1], (D, ATT), D ** -0.5, 0.109375, ((1, 32),)),
        "w_out": normal_values(seeds[2], (ATT, D), ATT ** -0.5, 0.125, ((1, 32),)),
        "maps": jnp.clip(jnp.exp(math.log(0.099609375) - 4.6018058 * jax.random.uniform(seeds[3], (HEADS, QBLOCKS, LIST, BLK, BLK), jnp.float32) ** block_scale(seeds[3], (HEADS, QBLOCKS, LIST, BLK, BLK), ((1, 16),), -0.2, 0.2)), 0.0009994507, 0.099609375).astype(jnp.bfloat16),
        "lists": draw_lists(jax.random.fold_in(seeds[5], 71), 0),
    }


def reference(features, w_value, w_out, maps, lists):
    values = jnp.dot(features, w_value, preferred_element_type=jnp.float32).astype(jnp.bfloat16)
    blocks = values.reshape(KBLOCKS, BLK, HEADS, HEAD_DIM)

    def one_head(head):
        head_values = lax.dynamic_index_in_dim(blocks, head, 2, keepdims=False)
        head_lists = lax.dynamic_index_in_dim(lists, head, 0, keepdims=False).astype(jnp.int32)
        chosen = jnp.take(head_values, head_lists, axis=0)
        head_maps = lax.dynamic_index_in_dim(maps, head, 0, keepdims=False)
        return jnp.einsum("qsij,qsjd->qid", head_maps.astype(jnp.float32), chosen.astype(jnp.float32))

    per_head = lax.map(one_head, jnp.arange(HEADS, dtype=jnp.int32))
    attn = per_head.transpose(1, 2, 0, 3).reshape(QBLOCKS * BLK, HEADS * HEAD_DIM).astype(jnp.bfloat16)
    return jnp.dot(attn, w_out, preferred_element_type=jnp.float32).astype(jnp.bfloat16)
```

```python
import jax
import jax.numpy as jnp
from jax import lax
from jax.experimental import pallas as pl
from jax.experimental.pallas import tpu as pltpu
from jax.sharding import Mesh, PartitionSpec as P

BLK = 128
NX = 4
NY = 4
BF = jnp.bfloat16
F32 = jnp.float32


def shift(n, k):
    return [(i, (i + k) % n) for i in range(n)]


def project(idx, pos, w0, w1, w2, w3, *rest):
    chunks, out, gath, wall = rest[:8], rest[8], rest[9], rest[10]
    rows = chunks[0].shape[0]
    width = w0.shape[0]
    for i, chunk in enumerate(chunks):
        at = pl.multiple_of(pos[i] * rows, rows)
        gath[pl.ds(at, rows), :] = chunk[...]
    for i, w in enumerate((w0, w1, w2, w3)):
        at = pl.multiple_of(pos[8 + i] * width, width)
        wall[pl.ds(at, width), :] = w[...]
    queries = out.shape[1]
    vals = jnp.dot(wall[...], gath[...], preferred_element_type=F32).astype(BF)
    rest[11][...] = vals
    for x in range(NX):
        for q in range(queries):
            at = pl.multiple_of(idx[x, q] * BLK, BLK)
            out[x, q] = rest[11][x * width : (x + 1) * width, pl.ds(at, BLK)]


def attend(src, got, maps, out):
    acc = jnp.zeros(out.shape[1:], F32)
    for s in range(maps.shape[0]):
        acc += lax.dot_general(
            got[src[s]], maps[s], (((1,), (1,)), ((), ())), preferred_element_type=F32
        )
    acc = acc.astype(BF)
    for k in range(out.shape[0]):
        out[k] = acc


def vmem(n):
    return [pl.BlockSpec(memory_space=pltpu.VMEM)] * n


def smem(n):
    return [pl.BlockSpec(memory_space=pltpu.SMEM)] * n


def body(features, w_value, w_out, maps, lists):
    kv_rows, feat = features.shape
    width = w_value.shape[1]
    x, y, core = (lax.axis_index(a) for a in ("x", "y", "core"))
    frame = lax.axis_index("frame")
    frames = lax.axis_size("frame")
    blocks_dev = kv_rows // BLK
    head = x * NY + y

    ft = features.T
    wt = w_value.T
    far = [lax.ppermute(ft, "y", shift(NY, k)) for k in (1, 3, 2)]
    wx = wt.reshape(width, NX, NY * 2 * feat)

    def w_to(k):
        return lax.dynamic_index_in_dim(wx, lax.rem(x + k, NX), 1, keepdims=False)

    wfar = [lax.ppermute(w_to(k), "x", shift(NX, k)) for k in (1, 3, 2)]
    mine = [ft] + far
    other = [lax.ppermute(c, "core", shift(2, 1)) for c in mine]
    ys = [y] + [lax.rem(y + NY - k, NY) for k in (1, 3, 2)]
    xs = [x] + [lax.rem(x + NX - k, NX) for k in (1, 3, 2)]
    pos = [2 * v + core for v in ys] + [2 * v + 1 - core for v in ys] + xs
    pos = jnp.stack(pos).astype(jnp.int32)

    here = lax.dynamic_index_in_dim(lists.reshape((NX, NY) + lists.shape[1:]), y, 1, keepdims=False)
    hit = here // blocks_dev == frame
    idx = jnp.sum(jnp.where(hit, here - frame * blocks_dev, 0), axis=2).astype(jnp.int32)
    queries = idx.shape[1]

    part = pl.pallas_call(
        project,
        out_shape=jax.ShapeDtypeStruct((NX, queries, width, BLK), BF),
        in_specs=smem(2) + vmem(12),
        out_specs=pl.BlockSpec(memory_space=pltpu.VMEM),
        scratch_shapes=[
            pltpu.VMEM((NY * 2 * feat, kv_rows), BF),
            pltpu.VMEM((NX * width, NY * 2 * feat), BF),
            pltpu.VMEM((NX * width, kv_rows), BF),
        ],
        compiler_params=pltpu.CompilerParams(vmem_limit_bytes=48 * 2**20),
        name="project",
    )(idx, pos, w_to(0), *wfar, *mine, *other)

    part = lax.all_to_all(part, "x", 0, 0, tiled=True)
    blocks = jnp.sum(part.astype(F32), axis=0).astype(BF)
    got = lax.all_to_all(blocks, "frame", 0, 0, tiled=True)

    my_list = lax.dynamic_slice(lists, (head, frame, 0), (1, 1, lists.shape[2])).reshape(-1)
    my_maps = lax.dynamic_index_in_dim(maps[:, 0], head, 0, keepdims=False)
    attn = pl.pallas_call(
        attend,
        out_shape=jax.ShapeDtypeStruct((NX * NY, width, BLK), BF),
        in_specs=smem(1) + vmem(2),
        out_specs=pl.BlockSpec(memory_space=pltpu.VMEM),
        name="attend",
    )((my_list // blocks_dev).astype(jnp.int32), got, my_maps)
    attn = lax.all_to_all(attn, ("x", "y"), 0, 0, tiled=True)
    attn = lax.all_gather(attn.reshape(NX * NY * width, BLK), "core", axis=0, tiled=True)
    wo = w_out.T.reshape(w_out.shape[1], NX * NY, 2, width).transpose(0, 2, 1, 3)
    mixed = jnp.dot(wo.reshape(w_out.shape[1], -1), attn, preferred_element_type=F32)
    return mixed.astype(BF).T


def solution(mesh):
    chan = ("x", "y", "core")
    grid = Mesh(mesh.devices.reshape(-1, NX, NY, 2), ("frame",) + chan)
    in_specs = (
        P("frame", chan),
        P(None, chan),
        P(None, chan),
        P(None, "frame", None, None, None),
        P(),
    )
    return jax.shard_map(body, mesh=grid, in_specs=in_specs, out_specs=P("frame", chan), check_vma=False)
```

```python
import jax
import jax.numpy as jnp
from jax import lax
from jax.experimental import pallas as pl
from jax.experimental.pallas import tpu as pltpu
from jax.sharding import Mesh, PartitionSpec as P

BLK = 128
NX = 4
NY = 4
BF = jnp.bfloat16
F32 = jnp.float32


def shift(n, k):
    return [(i, (i + k) % n) for i in range(n)]


def project(idx, pos, wall, *rest):
    chunks, out, gath, vals = rest[:8], rest[8], rest[9], rest[10]
    rows = chunks[0].shape[0]
    width = wall.shape[1]
    for i, chunk in enumerate(chunks):
        at = pl.multiple_of(pos[i] * rows, rows)
        gath[pl.ds(at, rows), :] = chunk[...]
    queries = out.shape[1]
    w = wall[...].reshape(NX * width, wall.shape[2])
    vals[...] = jnp.dot(w, gath[...], preferred_element_type=F32).astype(BF)
    for x in range(NX):
        for q in range(queries):
            at = pl.multiple_of(idx[x, q] * BLK, BLK)
            out[x, q] = vals[x * width : (x + 1) * width, pl.ds(at, BLK)]


def attend(src, got, maps, out):
    acc = jnp.zeros(out.shape[1:], F32)
    for s in range(maps.shape[0]):
        acc += lax.dot_general(
            got[src[s]], maps[s], (((1,), (1,)), ((), ())), preferred_element_type=F32
        )
    acc = acc.astype(BF)
    for k in range(out.shape[0]):
        out[k] = acc


def gate(x, *after):
    return pl.pallas_call(
        lambda *refs: None,
        out_shape=jax.ShapeDtypeStruct(x.shape, x.dtype),
        in_specs=[pl.BlockSpec(memory_space=pl.ANY)] * (1 + len(after)),
        out_specs=pl.BlockSpec(memory_space=pl.ANY),
        input_output_aliases={0: 0},
        compiler_params=pltpu.CompilerParams(vmem_limit_bytes=2**20),
        name="gate",
    )(x, *after)


def vmem(n):
    return [pl.BlockSpec(memory_space=pltpu.VMEM)] * n


def smem(n):
    return [pl.BlockSpec(memory_space=pltpu.SMEM)] * n


def body(features, w_value, w_out, maps, lists):
    kv_rows, feat = features.shape
    width = w_value.shape[1]
    x, y, core = (lax.axis_index(a) for a in ("x", "y", "core"))
    frame = lax.axis_index("frame")
    frames = lax.axis_size("frame")
    blocks_dev = kv_rows // BLK
    head = x * NY + y

    ft = features.T
    wt = w_value.T
    far = [lax.ppermute(ft, "y", shift(NY, k)) for k in (1, 3, 2)]
    wall = wt.reshape(width, NX, NY * 2 * feat).transpose(1, 0, 2)
    wall = lax.all_to_all(wall, "x", 0, 0, tiled=True)
    far[0] = gate(far[0], wall)
    mine = [ft] + far
    other = [lax.ppermute(c, "core", shift(2, 1)) for c in mine]
    ys = [y] + [lax.rem(y + NY - k, NY) for k in (1, 3, 2)]
    pos = [2 * v + core for v in ys] + [2 * v + 1 - core for v in ys]
    pos = jnp.stack(pos).astype(jnp.int32)

    here = lax.dynamic_index_in_dim(lists.reshape((NX, NY) + lists.shape[1:]), y, 1, keepdims=False)
    hit = here // blocks_dev == frame
    idx = jnp.sum(jnp.where(hit, here - frame * blocks_dev, 0), axis=2).astype(jnp.int32)
    queries = idx.shape[1]

    part = pl.pallas_call(
        project,
        out_shape=jax.ShapeDtypeStruct((NX, queries, width, BLK), BF),
        in_specs=smem(2) + vmem(9),
        out_specs=pl.BlockSpec(memory_space=pltpu.VMEM),
        scratch_shapes=[
            pltpu.VMEM((NY * 2 * feat, kv_rows), BF),
            pltpu.VMEM((NX * width, kv_rows), BF),
        ],
        compiler_params=pltpu.CompilerParams(vmem_limit_bytes=20 * 2**20),
        name="project",
    )(idx, pos, wall, *mine, *other)

    part = lax.all_to_all(part, "x", 0, 0, tiled=True)
    blocks = jnp.sum(part.astype(F32), axis=0).astype(BF)
    got = lax.all_to_all(blocks, "frame", 0, 0, tiled=True)

    my_list = lax.dynamic_slice(lists, (head, frame, 0), (1, 1, lists.shape[2])).reshape(-1)
    my_maps = lax.dynamic_index_in_dim(maps[:, 0], head, 0, keepdims=False)
    attn = pl.pallas_call(
        attend,
        out_shape=jax.ShapeDtypeStruct((NX * NY, width, BLK), BF),
        in_specs=smem(1) + vmem(2),
        out_specs=pl.BlockSpec(memory_space=pltpu.VMEM),
        compiler_params=pltpu.CompilerParams(vmem_limit_bytes=4 * 2**20),
        name="attend",
    )((my_list // blocks_dev).astype(jnp.int32), got, my_maps)
    attn = lax.all_to_all(attn, ("x", "y"), 0, 0, tiled=True)
    attn = lax.all_gather(attn.reshape(NX * NY * width, BLK), "core", axis=0, tiled=True)
    wo = w_out.T.reshape(w_out.shape[1], NX * NY, 2, width).transpose(0, 2, 1, 3)
    mixed = jnp.dot(wo.reshape(w_out.shape[1], -1), attn, preferred_element_type=F32)
    return mixed.astype(BF).T


def solution(mesh):
    chan = ("x", "y", "core")
    grid = Mesh(mesh.devices.reshape(-1, NX, NY, 2), ("frame",) + chan)
    in_specs = (
        P("frame", chan),
        P(None, chan),
        P(None, chan),
        P(None, "frame", None, None, None),
        P(),
    )
    return jax.shard_map(body, mesh=grid, in_specs=in_specs, out_specs=P("frame", chan), check_vma=False)
```

```python
import jax
import jax.numpy as jnp
from jax import lax
from jax.experimental import pallas as pl
from jax.experimental.pallas import tpu as pltpu
from jax.sharding import PartitionSpec as P

BLK = 128
SIDE = 4
CORES = 2
BF = jnp.bfloat16
F32 = jnp.float32
R4 = range(SIDE)


def at(x, y, core):
    return ((x % SIDE) * SIDE + y % SIDE) * CORES + core


ALL = [(x, y, c) for x in R4 for y in R4 for c in range(CORES)]
SWAP = [(at(x, y, c), at(x, y, 1 - c)) for x, y, c in ALL]
CROSS = [[at(x, y, 0) for x in R4] for y in R4] + [[at(x, y, 1) for y in R4] for x in R4]
PLANE = [[at(x, y, c) for x in R4 for y in R4] for c in range(CORES)]
PAIRS = [[at(x, y, c) for c in range(CORES)] for x in R4 for y in R4]


def along(k):
    return [(at(x, y, c), at(x, y + k, c) if c == 0 else at(x + k, y, c)) for x, y, c in ALL]


def pack(core, w, own, oth):
    feat = w.shape[1] // (SIDE * SIDE * CORES)

    def cuts(side, a):
        chips = [a * SIDE + b if side == 0 else b * SIDE + a for b in R4]
        starts = [(chip * CORES + side) * feat for chip in chips]
        return jnp.concatenate([w[:, s : s + feat] for s in starts], axis=1)

    for side in range(CORES):

        @pl.when(core[0] == side)
        def _(side=side):
            for a in R4:
                own[a] = cuts(side, a)
                oth[a] = cuts(1 - side, a)


def project(idx, pos, wall, *rest):
    chunks, (out, gath, vals) = rest[:-3], rest[-3:]
    for i, chunk in enumerate(chunks):
        rows = chunk.shape[0]
        gath[pl.ds(pl.multiple_of(pos[i] * rows, rows), rows), :] = chunk[...]
    for a in R4:
        w = wall[a].reshape(-1, wall.shape[3])
        vals[...] = jnp.dot(w, gath[...], preferred_element_type=F32).astype(BF)
        for q in range(out.shape[1]):
            out[a, q] = vals[:, pl.ds(pl.multiple_of(idx[a, q] * BLK, BLK), BLK)]


def fold(part, own, oth):
    width = own.shape[1]
    for q in range(own.shape[0]):
        total = part[0, q].astype(F32)
        for a in R4[1:]:
            total += part[a, q].astype(F32)
        own[q] = total[:width]
        oth[q] = total[width:].astype(BF)


def attend(src, got, maps, out):
    acc = jnp.zeros(out.shape[1:], F32)
    for s in range(maps.shape[0]):
        acc += lax.dot_general(
            got[src[s]], maps[s], (((1,), (1,)), ((), ())), preferred_element_type=F32
        )
    acc = acc.astype(BF)
    for k in range(out.shape[0]):
        out[k] = acc


def vmem(n):
    return [pl.BlockSpec(memory_space=pltpu.VMEM)] * n


def smem(n):
    return [pl.BlockSpec(memory_space=pltpu.SMEM)] * n


def limit(mib):
    return pltpu.CompilerParams(vmem_limit_bytes=mib * 2**20)


def body(features, w_value, w_out, maps, lists):
    kv_rows, feat = features.shape
    width = w_value.shape[1]
    chan = lax.axis_index("chan")
    frame = lax.axis_index("frame")
    x, y, core = chan // (SIDE * CORES), chan // CORES % SIDE, chan % CORES
    b = jnp.where(core == 0, y, x)
    blocks_dev = kv_rows // BLK
    head = chan // CORES

    def send(v, perm):
        return lax.ppermute(v, "chan", perm)

    def trade(v, groups):
        return lax.all_to_all(v, "chan", 0, 0, axis_index_groups=groups, tiled=True)

    ft = features.T
    chunks = [ft] + [send(ft, along(k)) for k in (1, 3, 2)]
    pos = jnp.stack([lax.rem(b + SIDE - k, SIDE) for k in (0, 1, 3, 2)]).astype(jnp.int32)

    half = jax.ShapeDtypeStruct((SIDE, width, SIDE * feat), BF)
    wown, woth = pl.pallas_call(
        pack,
        out_shape=(half, half),
        in_specs=smem(1) + vmem(1),
        out_specs=vmem(2),
        compiler_params=limit(4),
        name="pack",
    )(core.reshape(1).astype(jnp.int32), w_value.T)
    wall = trade(jnp.stack([wown, send(woth, SWAP)], axis=1), CROSS)

    grid = lists.reshape((SIDE, SIDE) + lists.shape[1:])
    here = jnp.where(
        core == 0,
        lax.dynamic_index_in_dim(grid, b, 1, keepdims=False),
        lax.dynamic_index_in_dim(grid, b, 0, keepdims=False),
    )
    hit = here // blocks_dev == frame
    idx = jnp.sum(jnp.where(hit, here - frame * blocks_dev, 0), axis=2).astype(jnp.int32)

    part = pl.pallas_call(
        project,
        out_shape=jax.ShapeDtypeStruct((SIDE, idx.shape[1], CORES * width, BLK), BF),
        in_specs=smem(2) + vmem(5),
        out_specs=vmem(1)[0],
        scratch_shapes=[pltpu.VMEM((SIDE * feat, kv_rows), BF), pltpu.VMEM((CORES * width, kv_rows), BF)],
        compiler_params=limit(20),
        name="project",
    )(idx, pos, wall, *chunks)
    part = trade(part, CROSS)
    side = (part.shape[1], width, BLK)
    mine, other = pl.pallas_call(
        fold,
        out_shape=(jax.ShapeDtypeStruct(side, F32), jax.ShapeDtypeStruct(side, BF)),
        in_specs=vmem(1),
        out_specs=vmem(2),
        compiler_params=limit(8),
        name="fold",
    )(part)
    blocks = (mine + send(other, SWAP).astype(F32)).astype(BF)
    got = lax.all_to_all(blocks, "frame", 0, 0, tiled=True)

    my_list = lax.dynamic_slice(lists, (head, frame, 0), (1, 1, lists.shape[2])).reshape(-1)
    my_maps = lax.dynamic_index_in_dim(maps[:, 0], head, 0, keepdims=False)
    attn = pl.pallas_call(
        attend,
        out_shape=jax.ShapeDtypeStruct((SIDE * SIDE, width, BLK), BF),
        in_specs=smem(1) + vmem(2),
        out_specs=vmem(1)[0],
        compiler_params=limit(4),
        name="attend",
    )((my_list // blocks_dev).astype(jnp.int32), got, my_maps)
    attn = trade(attn, PLANE).reshape(SIDE * SIDE * width, BLK)
    attn = lax.all_gather(attn, "chan", axis=0, tiled=True, axis_index_groups=PAIRS)
    wo = w_out.T.reshape(w_out.shape[1], SIDE * SIDE, CORES, width).transpose(0, 2, 1, 3)
    mixed = jnp.dot(wo.reshape(w_out.shape[1], -1), attn, preferred_element_type=F32)
    return mixed.astype(BF).T


def solution(mesh):
    in_specs = (
        P("frame", "chan"),
        P(None, "chan"),
        P(None, "chan"),
        P(None, "frame", None, None, None),
        P(),
    )
    return jax.shard_map(body, mesh=mesh, in_specs=in_specs, out_specs=P("frame", "chan"), check_vma=False)
```

```python
import jax
import jax.numpy as jnp
from jax import lax
from jax.experimental import pallas as pl
from jax.experimental.pallas import tpu as pltpu
from jax.sharding import PartitionSpec as P

BLK = 128
SIDE = 4
CORES = 2
BF = jnp.bfloat16
F32 = jnp.float32
R4 = range(SIDE)


def at(x, y, core):
    return ((x % SIDE) * SIDE + y % SIDE) * CORES + core


ALL = [(x, y, c) for x in R4 for y in R4 for c in range(CORES)]
SWAP = [(at(x, y, c), at(x, y, 1 - c)) for x, y, c in ALL]
CROSS = [[at(x, y, 0) for x in R4] for y in R4] + [[at(x, y, 1) for y in R4] for x in R4]
PLANE = [[at(x, y, c) for x in R4 for y in R4] for c in range(CORES)]
PAIRS = [[at(x, y, c) for c in range(CORES)] for x in R4 for y in R4]


def along(k):
    return [(at(x, y, c), at(x, y + k, c) if c == 0 else at(x + k, y, c)) for x, y, c in ALL]


def pack(core, w, own, oth):
    feat = w.shape[1] // (SIDE * SIDE * CORES)

    def cuts(side, a):
        chips = [a * SIDE + b if side == 0 else b * SIDE + a for b in R4]
        starts = [(chip * CORES + side) * feat for chip in chips]
        return jnp.concatenate([w[:, s : s + feat] for s in starts], axis=1)

    for side in range(CORES):

        @pl.when(core[0] == side)
        def _(side=side):
            for a in R4:
                own[a] = cuts(side, a)
                oth[a] = cuts(1 - side, a)


def project(idx, pos, wall, *rest):
    chunks, (out, gath, vals) = rest[:-3], rest[-3:]
    for i, chunk in enumerate(chunks):
        rows = chunk.shape[0]
        gath[pl.ds(pl.multiple_of(pos[i] * rows, rows), rows), :] = chunk[...]
    for a in R4:
        w = wall[a].reshape(-1, wall.shape[3])
        vals[...] = jnp.dot(w, gath[...], preferred_element_type=F32).astype(BF)
        for q in range(out.shape[1]):
            out[a, q] = vals[:, pl.ds(pl.multiple_of(idx[a, q] * BLK, BLK), BLK)]


def fold(part, own, oth):
    width = own.shape[1]
    for q in range(own.shape[0]):
        total = part[0, q].astype(F32)
        for a in R4[1:]:
            total += part[a, q].astype(F32)
        own[q] = total[:width]
        oth[q] = total[width:].astype(BF)


def attend(src, got, maps, out):
    acc = jnp.zeros(out.shape[1:], F32)
    for s in range(maps.shape[0]):
        acc += lax.dot_general(
            got[src[s]], maps[s], (((1,), (1,)), ((), ())), preferred_element_type=F32
        )
    acc = acc.astype(BF)
    for k in range(out.shape[0]):
        out[k] = acc


def hold(xs):
    whole = [pl.BlockSpec(memory_space=pl.ANY)] * len(xs)
    return pl.pallas_call(
        lambda *refs: None,
        out_shape=[jax.ShapeDtypeStruct(x.shape, x.dtype) for x in xs],
        in_specs=whole,
        out_specs=whole,
        input_output_aliases={i: i for i in range(len(xs))},
        cost_estimate=pl.CostEstimate(flops=2 * 10**10, bytes_accessed=10**7, transcendentals=0),
        compiler_params=limit(1),
        name="hold",
    )(*xs)


def vmem(n):
    return [pl.BlockSpec(memory_space=pltpu.VMEM)] * n


def smem(n):
    return [pl.BlockSpec(memory_space=pltpu.SMEM)] * n


def limit(mib):
    return pltpu.CompilerParams(vmem_limit_bytes=mib * 2**20)


def body(features, w_value, w_out, maps, lists):
    kv_rows, feat = features.shape
    width = w_value.shape[1]
    chan = lax.axis_index("chan")
    frame = lax.axis_index("frame")
    x, y, core = chan // (SIDE * CORES), chan // CORES % SIDE, chan % CORES
    b = jnp.where(core == 0, y, x)
    blocks_dev = kv_rows // BLK
    head = chan // CORES

    def send(v, perm):
        return lax.ppermute(v, "chan", perm)

    def trade(v, groups):
        return lax.all_to_all(v, "chan", 0, 0, axis_index_groups=groups, tiled=True)

    ft = features.T
    chunks = [ft, *hold([send(ft, along(k)) for k in (1, 3, 2)])]
    pos = jnp.stack([lax.rem(b + SIDE - k, SIDE) for k in (0, 1, 3, 2)]).astype(jnp.int32)

    half = jax.ShapeDtypeStruct((SIDE, width, SIDE * feat), BF)
    wown, woth = pl.pallas_call(
        pack,
        out_shape=(half, half),
        in_specs=smem(1) + vmem(1),
        out_specs=vmem(2),
        compiler_params=limit(4),
        name="pack",
    )(core.reshape(1).astype(jnp.int32), w_value.T)
    wall = trade(jnp.stack([wown, send(woth, SWAP)], axis=1), CROSS)

    grid = lists.reshape((SIDE, SIDE) + lists.shape[1:])
    here = jnp.where(
        core == 0,
        lax.dynamic_index_in_dim(grid, b, 1, keepdims=False),
        lax.dynamic_index_in_dim(grid, b, 0, keepdims=False),
    )
    hit = here // blocks_dev == frame
    idx = jnp.sum(jnp.where(hit, here - frame * blocks_dev, 0), axis=2).astype(jnp.int32)

    part = pl.pallas_call(
        project,
        out_shape=jax.ShapeDtypeStruct((SIDE, idx.shape[1], CORES * width, BLK), BF),
        in_specs=smem(2) + vmem(5),
        out_specs=vmem(1)[0],
        scratch_shapes=[pltpu.VMEM((SIDE * feat, kv_rows), BF), pltpu.VMEM((CORES * width, kv_rows), BF)],
        compiler_params=limit(20),
        name="project",
    )(idx, pos, wall, *chunks)
    part = trade(part, CROSS)
    side = (part.shape[1], width, BLK)
    mine, other = pl.pallas_call(
        fold,
        out_shape=(jax.ShapeDtypeStruct(side, F32), jax.ShapeDtypeStruct(side, BF)),
        in_specs=vmem(1),
        out_specs=vmem(2),
        compiler_params=limit(8),
        name="fold",
    )(part)
    blocks = (mine + send(other, SWAP).astype(F32)).astype(BF)
    got = lax.all_to_all(blocks, "frame", 0, 0, tiled=True)

    my_list = lax.dynamic_slice(lists, (head, frame, 0), (1, 1, lists.shape[2])).reshape(-1)
    my_maps = lax.dynamic_index_in_dim(maps[:, 0], head, 0, keepdims=False)
    attn = pl.pallas_call(
        attend,
        out_shape=jax.ShapeDtypeStruct((SIDE * SIDE, width, BLK), BF),
        in_specs=smem(1) + vmem(2),
        out_specs=vmem(1)[0],
        compiler_params=limit(4),
        name="attend",
    )((my_list // blocks_dev).astype(jnp.int32), got, my_maps)
    attn = trade(attn, PLANE).reshape(SIDE * SIDE * width, BLK)
    attn = lax.all_gather(attn, "chan", axis=0, tiled=True, axis_index_groups=PAIRS)
    wo = w_out.T.reshape(w_out.shape[1], SIDE * SIDE, CORES, width).transpose(0, 2, 1, 3)
    mixed = jnp.dot(wo.reshape(w_out.shape[1], -1), attn, preferred_element_type=F32)
    return mixed.astype(BF).T


def solution(mesh):
    in_specs = (
        P("frame", "chan"),
        P(None, "chan"),
        P(None, "chan"),
        P(None, "frame", None, None, None),
        P(),
    )
    return jax.shard_map(body, mesh=mesh, in_specs=in_specs, out_specs=P("frame", "chan"), check_vma=False)
```

```python
import functools

import jax
import jax.numpy as jnp
from jax import lax
from jax.experimental import pallas as pl
from jax.experimental.pallas import tpu as pltpu
from jax.sharding import PartitionSpec as P

BLK = 128
SIDE = 4
CORES = 2
BF = jnp.bfloat16
F32 = jnp.float32
R4 = range(SIDE)


def at(x, y, core):
    return ((x % SIDE) * SIDE + y % SIDE) * CORES + core


ALL = [(x, y, c) for x in R4 for y in R4 for c in range(CORES)]
SWAP = [(at(x, y, c), at(x, y, 1 - c)) for x, y, c in ALL]
CROSS = [[at(x, y, 0) for x in R4] for y in R4] + [[at(x, y, 1) for y in R4] for x in R4]
PLANE = [[at(x, y, c) for x in R4 for y in R4] for c in range(CORES)]
PAIRS = [[at(x, y, c) for c in range(CORES)] for x in R4 for y in R4]


def along(k):
    return [(at(x, y, c), at(x, y + k, c) if c == 0 else at(x + k, y, c)) for x, y, c in ALL]


def pack(core, w, own, oth):
    feat = w.shape[1] // (SIDE * SIDE * CORES)

    def cuts(side, a):
        chips = [a * SIDE + b if side == 0 else b * SIDE + a for b in R4]
        starts = [(chip * CORES + side) * feat for chip in chips]
        return jnp.concatenate([w[:, s : s + feat] for s in starts], axis=1)

    for side in range(CORES):

        @pl.when(core[0] == side)
        def _(side=side):
            for a in R4:
                own[a] = cuts(side, a)
                oth[a] = cuts(1 - side, a)


def prepare(blocks_dev, pos, lists, maps, idx, src, mine, sem):
    core, b, head, frame = (pos[i] for i in range(4))
    copy = pltpu.make_async_copy(maps.at[head, 0], mine, sem)
    copy.start()
    for a in R4:
        partner = jnp.where(core == 0, a * SIDE + b, b * SIDE + a)
        for q in range(idx.shape[1]):
            place = jnp.int32(0)
            for s in range(lists.shape[1]):
                local = lists[partner, s, q] - frame * blocks_dev
                place = jnp.where((local >= 0) & (local < blocks_dev), local, place)
            idx[a, q] = place
    for s in range(lists.shape[1]):
        src[s] = lax.div(lists[head, s, frame], jnp.int32(blocks_dev))
    copy.wait()


def project(idx, pos, wall, *rest):
    chunks, (out, gath, vals) = rest[:-3], rest[-3:]
    for i, chunk in enumerate(chunks):
        rows = chunk.shape[0]
        gath[pl.ds(pl.multiple_of(pos[i] * rows, rows), rows), :] = chunk[...]
    for a in R4:
        w = wall[a].reshape(-1, wall.shape[3])
        vals[...] = jnp.dot(w, gath[...], preferred_element_type=F32).astype(BF)
        for q in range(out.shape[1]):
            out[a, q] = vals[:, pl.ds(pl.multiple_of(idx[a, q] * BLK, BLK), BLK)]


def fold(part, own, oth):
    width = own.shape[1]
    for q in range(own.shape[0]):
        total = part[0, q].astype(F32)
        for a in R4[1:]:
            total += part[a, q].astype(F32)
        own[q] = total[:width]
        oth[q] = total[width:].astype(BF)


def merge(core, mine, pair, out):
    out[...] = (mine[...] + pair[1 - core[0]].astype(F32)).astype(BF)


def attend(src, got, maps, out):
    acc = jnp.zeros(out.shape[1:], F32)
    for s in range(maps.shape[0]):
        acc += lax.dot_general(
            got[src[s]], maps[s], (((1,), (1,)), ((), ())), preferred_element_type=F32
        )
    acc = acc.astype(BF)
    for k in range(out.shape[0]):
        out[k] = acc


def output(attn, w, out):
    rows = [attn[c, chip] for chip in range(attn.shape[1]) for c in range(CORES)]
    out[...] = jnp.dot(w[...], jnp.concatenate(rows, axis=0), preferred_element_type=F32).astype(BF)


def vmem(n):
    return [pl.BlockSpec(memory_space=pltpu.VMEM)] * n


def smem(n):
    return [pl.BlockSpec(memory_space=pltpu.SMEM)] * n


def limit(mib):
    return pltpu.CompilerParams(vmem_limit_bytes=mib * 2**20)


def body(features, w_value, w_out, maps, lists):
    kv_rows, feat = features.shape
    width = w_value.shape[1]
    chan = lax.axis_index("chan")
    frame = lax.axis_index("frame")
    x, y, core = chan // (SIDE * CORES), chan // CORES % SIDE, chan % CORES
    b = jnp.where(core == 0, y, x)
    head = chan // CORES

    def send(v, perm):
        return lax.ppermute(v, "chan", perm)

    def trade(v, groups):
        return lax.all_to_all(v, "chan", 0, 0, axis_index_groups=groups, tiled=True)

    ft = features.T
    chunks = [ft] + [send(ft, along(k)) for k in (1, 3, 2)]
    pos = jnp.stack([lax.rem(b + SIDE - k, SIDE) for k in (0, 1, 3, 2)]).astype(jnp.int32)

    half = jax.ShapeDtypeStruct((SIDE, width, SIDE * feat), BF)
    wown, woth = pl.pallas_call(
        pack,
        out_shape=(half, half),
        in_specs=smem(1) + vmem(1),
        out_specs=vmem(2),
        compiler_params=limit(4),
        name="pack",
    )(core.reshape(1).astype(jnp.int32), w_value.T)
    wall = trade(jnp.stack([wown, send(woth, SWAP)], axis=1), CROSS)

    slots = lists.shape[2]
    idx, src, my_maps = pl.pallas_call(
        functools.partial(prepare, kv_rows // BLK),
        out_shape=(
            jax.ShapeDtypeStruct((SIDE, lists.shape[1]), jnp.int32),
            jax.ShapeDtypeStruct((slots,), jnp.int32),
            jax.ShapeDtypeStruct((slots, BLK, BLK), BF),
        ),
        in_specs=smem(2) + [pl.BlockSpec(memory_space=pltpu.HBM)],
        out_specs=smem(2) + vmem(1),
        scratch_shapes=[pltpu.SemaphoreType.DMA],
        compiler_params=limit(4),
        name="prepare",
    )(jnp.stack([core, b, head, frame]).astype(jnp.int32), lists.transpose(0, 2, 1), maps)

    part = pl.pallas_call(
        project,
        out_shape=jax.ShapeDtypeStruct((SIDE, idx.shape[1], CORES * width, BLK), BF),
        in_specs=smem(2) + vmem(5),
        out_specs=vmem(1)[0],
        scratch_shapes=[pltpu.VMEM((SIDE * feat, kv_rows), BF), pltpu.VMEM((CORES * width, kv_rows), BF)],
        compiler_params=limit(20),
        name="project",
    )(idx, pos, wall, *chunks)
    part = trade(part, CROSS)
    side = (part.shape[1], width, BLK)
    mine, other = pl.pallas_call(
        fold,
        out_shape=(jax.ShapeDtypeStruct(side, F32), jax.ShapeDtypeStruct(side, BF)),
        in_specs=vmem(1),
        out_specs=vmem(2),
        compiler_params=limit(8),
        name="fold",
    )(part)
    pair = lax.all_gather(other, "chan", axis_index_groups=PAIRS)
    blocks = pl.pallas_call(
        merge,
        out_shape=jax.ShapeDtypeStruct(side, BF),
        in_specs=smem(1) + vmem(2),
        out_specs=vmem(1)[0],
        compiler_params=limit(4),
        name="merge",
    )(core.reshape(1).astype(jnp.int32), mine, pair)
    got = lax.all_to_all(blocks, "frame", 0, 0, tiled=True)
    attn = pl.pallas_call(
        attend,
        out_shape=jax.ShapeDtypeStruct((SIDE * SIDE, width, BLK), BF),
        in_specs=smem(1) + vmem(2),
        out_specs=vmem(1)[0],
        compiler_params=limit(4),
        name="attend",
    )(src, got, my_maps)
    attn = lax.all_gather(trade(attn, PLANE), "chan", axis_index_groups=PAIRS)
    mixed = pl.pallas_call(
        output,
        out_shape=jax.ShapeDtypeStruct((w_out.shape[1], BLK), BF),
        in_specs=vmem(2),
        out_specs=vmem(1)[0],
        compiler_params=limit(4),
        name="output",
    )(attn, w_out.T)
    return mixed.T


def solution(mesh):
    in_specs = (
        P("frame", "chan"),
        P(None, "chan"),
        P(None, "chan"),
        P(None, "frame", None, None, None),
        P(),
    )
    return jax.shard_map(body, mesh=mesh, in_specs=in_specs, out_specs=P("frame", "chan"), check_vma=False)
```

```python
import functools

import jax
import jax.numpy as jnp
from jax import lax
from jax.experimental import pallas as pl
from jax.experimental.pallas import tpu as pltpu
from jax.sharding import PartitionSpec as P

BLK = 128
SIDE = 4
CORES = 2
BF = jnp.bfloat16
F32 = jnp.float32
R4 = range(SIDE)


def at(x, y, core):
    return ((x % SIDE) * SIDE + y % SIDE) * CORES + core


ALL = [(x, y, c) for x in R4 for y in R4 for c in range(CORES)]
CROSS = [[at(x, y, 0) for x in R4] for y in R4] + [[at(x, y, 1) for y in R4] for x in R4]
PLANE = [[at(x, y, c) for x in R4 for y in R4] for c in range(CORES)]
PAIRS = [[at(x, y, c) for c in range(CORES)] for x in R4 for y in R4]


def along(k):
    return [(at(x, y, c), at(x, y + k, c) if c == 0 else at(x + k, y, c)) for x, y, c in ALL]


def halve(core, both, out):
    size = out.shape[1]
    for c in range(CORES):

        @pl.when(core[0] == c)
        def _(start=c * (both.shape[2] - size)):
            out[...] = jnp.concatenate([both[i, :, start : start + size] for i in range(CORES)], axis=0)


def pack(core, w, out):
    span = w.shape[2] // SIDE
    piece = span // SIDE
    cols = jnp.concatenate([w[0], w[1]], axis=0)

    @pl.when(core[0] == 0)
    def _():
        for a in R4:
            out[a] = cols[:, a * span : (a + 1) * span]

    @pl.when(core[0] == 1)
    def _():
        for a in R4:
            starts = [(b * SIDE + a) * piece for b in R4]
            out[a] = jnp.concatenate([cols[:, s : s + piece] for s in starts], axis=1)


def prepare(blocks_dev, pos, lists, maps, idx, src, mine, sem):
    head, frame = pos[0], pos[1]
    copy = pltpu.make_async_copy(maps.at[head, 0], mine, sem)
    copy.start()
    for q in range(idx.shape[0]):
        place = jnp.int32(0)
        for s in range(lists.shape[1]):
            local = lists[head, s, q] - frame * blocks_dev
            place = jnp.where((local >= 0) & (local < blocks_dev), local, place)
        idx[q] = place
    for s in range(lists.shape[1]):
        src[s] = lax.div(lists[head, s, frame], jnp.int32(blocks_dev))
    copy.wait()


def project(pos, idx, wall, *rest):
    chunks, (out, gath) = rest[:-2], rest[-2:]
    for i, chunk in enumerate(chunks):
        rows = chunk.shape[0]
        gath[pl.ds(pl.multiple_of(pos[i] * rows, rows), rows), :] = chunk[...]
    w = wall[...].reshape(-1, wall.shape[2])
    out[...] = jnp.dot(w, gath[...], preferred_element_type=F32).astype(BF).reshape(out.shape)


def fold(first, core, idx, part, own, oth, vals):
    total = part[0].astype(F32)
    for a in R4[1:]:
        total += part[a].astype(F32)
    vals[...] = total.astype(BF)
    width = own.shape[1]
    mine = pl.ds(pl.multiple_of(core[0] * width, width), width)
    theirs = pl.ds(pl.multiple_of((1 - core[0]) * width, width), width)
    last = vals.shape[1] // BLK - 1
    for q in range(own.shape[0]):
        block = jnp.clip(idx[q] - core[0] * first, 0, last)
        at_q = pl.ds(pl.multiple_of(block * BLK, BLK), BLK)
        own[q] = vals[mine, at_q]
        oth[q] = vals[theirs, at_q]


def merge(half, core, idx, own, pair, out):
    for q in range(out.shape[0]):
        here = (idx[q] < half) == (core[0] == 0)

        @pl.when(here)
        def _(q=q):
            out[q] = own[q]

        @pl.when(jnp.logical_not(here))
        def _(q=q):
            out[q] = pair[1 - core[0], q]


def attend(src, got, maps, out):
    acc = jnp.zeros(out.shape[1:], F32)
    for s in range(maps.shape[0]):
        acc += lax.dot_general(
            got[src[s]], maps[s], (((1,), (1,)), ((), ())), preferred_element_type=F32
        )
    acc = acc.astype(BF)
    for k in range(out.shape[0]):
        out[k] = acc


def output(attn, w, out):
    rows = [attn[c, chip] for chip in range(attn.shape[1]) for c in range(CORES)]
    out[...] = jnp.dot(w[...], jnp.concatenate(rows, axis=0), preferred_element_type=F32).astype(BF)


def hold(xs):
    whole = [pl.BlockSpec(memory_space=pl.ANY)] * len(xs)
    return pl.pallas_call(
        lambda *refs: None,
        out_shape=[jax.ShapeDtypeStruct(x.shape, x.dtype) for x in xs],
        in_specs=whole,
        out_specs=whole,
        input_output_aliases={i: i for i in range(len(xs))},
        cost_estimate=pl.CostEstimate(flops=2 * 10**10, bytes_accessed=10**7, transcendentals=0),
        compiler_params=limit(1),
        name="hold",
    )(*xs)


def vmem(n):
    return [pl.BlockSpec(memory_space=pltpu.VMEM)] * n


def smem(n):
    return [pl.BlockSpec(memory_space=pltpu.SMEM)] * n


def limit(mib):
    return pltpu.CompilerParams(vmem_limit_bytes=mib * 2**20)


def body(features, w_value, w_out, maps, lists):
    kv_rows, feat = features.shape
    width = w_value.shape[1]
    chan = lax.axis_index("chan")
    frame = lax.axis_index("frame")
    x, y, core = chan // (SIDE * CORES), chan // CORES % SIDE, chan % CORES
    b = jnp.where(core == 0, y, x)
    head = chan // CORES

    def send(v, perm):
        return lax.ppermute(v, "chan", perm)

    def trade(v, groups):
        return lax.all_to_all(v, "chan", 0, 0, axis_index_groups=groups, tiled=True)

    def pair(v):
        return lax.all_gather(v, "chan", axis_index_groups=PAIRS)

    blocks_dev = kv_rows // BLK
    half = (blocks_dev + 1) // CORES
    one = core.reshape(1).astype(jnp.int32)
    both = pl.pallas_call(
        halve,
        out_shape=jax.ShapeDtypeStruct((CORES * feat, half * BLK), BF),
        in_specs=smem(1) + vmem(1),
        out_specs=vmem(1)[0],
        compiler_params=limit(4),
        name="halve",
    )(one, pair(features.T))
    chunks = [both, *hold([send(both, along(k)) for k in (1, 3, 2)])]
    pos = jnp.stack([lax.rem(b + SIDE - k, SIDE) for k in (0, 1, 3, 2)]).astype(jnp.int32)

    wall = pl.pallas_call(
        pack,
        out_shape=jax.ShapeDtypeStruct((SIDE, CORES * width, SIDE * CORES * feat), BF),
        in_specs=smem(1) + vmem(1),
        out_specs=vmem(1)[0],
        compiler_params=limit(4),
        name="pack",
    )(one, pair(w_value.T))
    wall = trade(wall, CROSS)

    queries, slots = lists.shape[1:]
    idx, src, my_maps = pl.pallas_call(
        functools.partial(prepare, blocks_dev),
        out_shape=(
            jax.ShapeDtypeStruct((queries,), jnp.int32),
            jax.ShapeDtypeStruct((slots,), jnp.int32),
            jax.ShapeDtypeStruct((slots, BLK, BLK), BF),
        ),
        in_specs=smem(2) + [pl.BlockSpec(memory_space=pltpu.HBM)],
        out_specs=smem(2) + vmem(1),
        scratch_shapes=[pltpu.SemaphoreType.DMA],
        compiler_params=limit(4),
        name="prepare",
    )(jnp.stack([head, frame]).astype(jnp.int32), lists.transpose(0, 2, 1), maps)

    part = pl.pallas_call(
        project,
        out_shape=jax.ShapeDtypeStruct((SIDE, CORES * width, half * BLK), BF),
        in_specs=smem(1) + [pl.BlockSpec(memory_space=pl.ANY)] + vmem(5),
        out_specs=vmem(1)[0],
        scratch_shapes=[pltpu.VMEM((SIDE * CORES * feat, half * BLK), BF)],
        compiler_params=limit(20),
        name="project",
    )(pos, idx, wall, *chunks)
    part = trade(part, CROSS)
    side = jax.ShapeDtypeStruct((queries, width, BLK), BF)
    own, oth = pl.pallas_call(
        functools.partial(fold, blocks_dev - half),
        out_shape=(side, side),
        in_specs=smem(2) + vmem(1),
        out_specs=vmem(2),
        scratch_shapes=[pltpu.VMEM((CORES * width, half * BLK), BF)],
        compiler_params=limit(8),
        name="fold",
    )(one, idx, part)
    blocks = pl.pallas_call(
        functools.partial(merge, half),
        out_shape=side,
        in_specs=smem(2) + vmem(2),
        out_specs=vmem(1)[0],
        compiler_params=limit(4),
        name="merge",
    )(one, idx, own, pair(oth))
    got = lax.all_to_all(blocks, "frame", 0, 0, tiled=True)
    attn = pl.pallas_call(
        attend,
        out_shape=jax.ShapeDtypeStruct((SIDE * SIDE, width, BLK), BF),
        in_specs=smem(1) + vmem(2),
        out_specs=vmem(1)[0],
        compiler_params=limit(4),
        name="attend",
    )(src, got, my_maps)
    attn = pair(trade(attn, PLANE))
    mixed = pl.pallas_call(
        output,
        out_shape=jax.ShapeDtypeStruct((w_out.shape[1], BLK), BF),
        in_specs=vmem(2),
        out_specs=vmem(1)[0],
        compiler_params=limit(4),
        name="output",
    )(attn, w_out.T)
    return mixed.T


def solution(mesh):
    in_specs = (
        P("frame", "chan"),
        P(None, "chan"),
        P(None, "chan"),
        P(None, "frame", None, None, None),
        P(),
    )
    return jax.shard_map(body, mesh=mesh, in_specs=in_specs, out_specs=P("frame", "chan"), check_vma=False)
```

```python
import functools

import jax
import jax.numpy as jnp
from jax import lax
from jax.experimental import pallas as pl
from jax.experimental.pallas import tpu as pltpu
from jax.sharding import PartitionSpec as P

BLK = 128
SIDE = 4
CORES = 2
BF = jnp.bfloat16
F32 = jnp.float32
R4 = range(SIDE)


def at(x, y, core):
    return ((x % SIDE) * SIDE + y % SIDE) * CORES + core


ALL = [(x, y, c) for x in R4 for y in R4 for c in range(CORES)]
CROSS = [[at(x, y, 0) for x in R4] for y in R4] + [[at(x, y, 1) for y in R4] for x in R4]
PLANE = [[at(x, y, c) for x in R4 for y in R4] for c in range(CORES)]
PAIRS = [[at(x, y, c) for c in range(CORES)] for x in R4 for y in R4]


def along(k):
    return [(at(x, y, c), at(x, y + k, c) if c == 0 else at(x + k, y, c)) for x, y, c in ALL]


def halve(core, both, out):
    size = out.shape[1]
    for c in range(CORES):

        @pl.when(core[0] == c)
        def _(start=c * (both.shape[2] - size)):
            out[...] = jnp.concatenate([both[i, :, start : start + size] for i in range(CORES)], axis=0)


def pack(core, w, out):
    span = w.shape[2] // SIDE
    piece = span // SIDE
    cols = jnp.concatenate([w[0], w[1]], axis=0)

    @pl.when(core[0] == 0)
    def _():
        for a in R4:
            out[a] = cols[:, a * span : (a + 1) * span]

    @pl.when(core[0] == 1)
    def _():
        for a in R4:
            starts = [(b * SIDE + a) * piece for b in R4]
            out[a] = jnp.concatenate([cols[:, s : s + piece] for s in starts], axis=1)


def prepare(blocks_dev, pos, lists, maps, idx, src, mine, sem):
    head, frame = pos[0], pos[1]
    copy = pltpu.make_async_copy(maps.at[head, 0], mine, sem)
    copy.start()
    for q in range(idx.shape[0]):
        place = jnp.int32(0)
        for s in range(lists.shape[1]):
            local = lists[head, s, q] - frame * blocks_dev
            place = jnp.where((local >= 0) & (local < blocks_dev), local, place)
        idx[q] = place
    for s in range(lists.shape[1]):
        src[s] = lax.div(lists[head, s, frame], jnp.int32(blocks_dev))
    copy.wait()


def project(pos, idx, wall, *rest):
    chunks, (out, gath) = rest[:-2], rest[-2:]
    for i, chunk in enumerate(chunks):
        rows = chunk.shape[0]
        gath[pl.ds(pl.multiple_of(pos[i] * rows, rows), rows), :] = chunk[...]
    w = wall[...].reshape(-1, wall.shape[2])
    out[...] = jnp.dot(w, gath[...], preferred_element_type=F32).astype(BF).reshape(out.shape)


def fold(blocks_dev, core, idx, part, own, oth, vals):
    total = part[0].astype(F32)
    for a in R4[1:]:
        total += part[a].astype(F32)
    vals[...] = total.astype(BF)
    width = own.shape[1]
    half = vals.shape[1] // BLK
    mine = pl.ds(pl.multiple_of(core[0] * width, width), width)
    theirs = pl.ds(pl.multiple_of((1 - core[0]) * width, width), width)
    for q in range(own.shape[0]):
        here = (idx[q] < half) == (core[0] == 0)
        block = jnp.clip(idx[q] - core[0] * (blocks_dev - half), 0, half - 1)
        at_q = pl.ds(pl.multiple_of(block * BLK, BLK), BLK)
        own[q] = jnp.where(here, vals[mine, at_q], jnp.zeros((), BF))
        oth[q] = jnp.where(here, vals[theirs, at_q], jnp.zeros((), BF))


def merge(core, own, pair, out):
    out[...] = own[...] + pair[1 - core[0]]


def attend(src, got, maps, out):
    acc = jnp.zeros(out.shape[1:], F32)
    for s in range(maps.shape[0]):
        acc += lax.dot_general(
            got[src[s]], maps[s], (((1,), (1,)), ((), ())), preferred_element_type=F32
        )
    acc = acc.astype(BF)
    for k in range(out.shape[0]):
        out[k] = acc


def output(attn, w, out):
    rows = [attn[c, chip] for chip in range(attn.shape[1]) for c in range(CORES)]
    out[...] = jnp.dot(w[...], jnp.concatenate(rows, axis=0), preferred_element_type=F32).astype(BF)


def hold(xs):
    whole = [pl.BlockSpec(memory_space=pl.ANY)] * len(xs)
    return pl.pallas_call(
        lambda *refs: None,
        out_shape=[jax.ShapeDtypeStruct(x.shape, x.dtype) for x in xs],
        in_specs=whole,
        out_specs=whole,
        input_output_aliases={i: i for i in range(len(xs))},
        cost_estimate=pl.CostEstimate(flops=2 * 10**10, bytes_accessed=10**7, transcendentals=0),
        compiler_params=limit(1),
        name="hold",
    )(*xs)


def vmem(n):
    return [pl.BlockSpec(memory_space=pltpu.VMEM)] * n


def smem(n):
    return [pl.BlockSpec(memory_space=pltpu.SMEM)] * n


def limit(mib):
    return pltpu.CompilerParams(vmem_limit_bytes=mib * 2**20)


def body(features, w_value, w_out, maps, lists):
    kv_rows, feat = features.shape
    width = w_value.shape[1]
    chan = lax.axis_index("chan")
    frame = lax.axis_index("frame")
    x, y, core = chan // (SIDE * CORES), chan // CORES % SIDE, chan % CORES
    b = jnp.where(core == 0, y, x)
    head = chan // CORES

    def send(v, perm):
        return lax.ppermute(v, "chan", perm)

    def trade(v, groups):
        return lax.all_to_all(v, "chan", 0, 0, axis_index_groups=groups, tiled=True)

    def pair(v):
        return lax.all_gather(v, "chan", axis_index_groups=PAIRS)

    blocks_dev = kv_rows // BLK
    half = (blocks_dev + 1) // CORES
    one = core.reshape(1).astype(jnp.int32)
    both = pl.pallas_call(
        halve,
        out_shape=jax.ShapeDtypeStruct((CORES * feat, half * BLK), BF),
        in_specs=smem(1) + vmem(1),
        out_specs=vmem(1)[0],
        compiler_params=limit(4),
        name="halve",
    )(one, pair(features.T))
    chunks = [both, *hold([send(both, along(k)) for k in (1, 3, 2)])]
    pos = jnp.stack([lax.rem(b + SIDE - k, SIDE) for k in (0, 1, 3, 2)]).astype(jnp.int32)

    wall = pl.pallas_call(
        pack,
        out_shape=jax.ShapeDtypeStruct((SIDE, CORES * width, SIDE * CORES * feat), BF),
        in_specs=smem(1) + vmem(1),
        out_specs=vmem(1)[0],
        compiler_params=limit(4),
        name="pack",
    )(one, pair(w_value.T))
    wall = trade(wall, CROSS)

    queries, slots = lists.shape[1:]
    idx, src, my_maps = pl.pallas_call(
        functools.partial(prepare, blocks_dev),
        out_shape=(
            jax.ShapeDtypeStruct((queries,), jnp.int32),
            jax.ShapeDtypeStruct((slots,), jnp.int32),
            jax.ShapeDtypeStruct((slots, BLK, BLK), BF),
        ),
        in_specs=smem(2) + [pl.BlockSpec(memory_space=pltpu.HBM)],
        out_specs=smem(2) + vmem(1),
        scratch_shapes=[pltpu.SemaphoreType.DMA],
        compiler_params=limit(4),
        name="prepare",
    )(jnp.stack([head, frame]).astype(jnp.int32), lists.transpose(0, 2, 1), maps)

    part = pl.pallas_call(
        project,
        out_shape=jax.ShapeDtypeStruct((SIDE, CORES * width, half * BLK), BF),
        in_specs=smem(1) + [pl.BlockSpec(memory_space=pl.ANY)] + vmem(5),
        out_specs=vmem(1)[0],
        scratch_shapes=[pltpu.VMEM((SIDE * CORES * feat, half * BLK), BF)],
        compiler_params=limit(20),
        name="project",
    )(pos, idx, wall, *chunks)
    part = trade(part, CROSS)
    side = jax.ShapeDtypeStruct((queries, width, BLK), BF)
    own, oth = pl.pallas_call(
        functools.partial(fold, blocks_dev),
        out_shape=(side, side),
        in_specs=smem(2) + vmem(1),
        out_specs=vmem(2),
        scratch_shapes=[pltpu.VMEM((CORES * width, half * BLK), BF)],
        compiler_params=limit(8),
        name="fold",
    )(one, idx, part)
    blocks = pl.pallas_call(
        merge,
        out_shape=side,
        in_specs=smem(1) + vmem(2),
        out_specs=vmem(1)[0],
        compiler_params=limit(4),
        name="merge",
    )(one, own, pair(oth))
    got = lax.all_to_all(blocks, "frame", 0, 0, tiled=True)
    attn = pl.pallas_call(
        attend,
        out_shape=jax.ShapeDtypeStruct((SIDE * SIDE, width, BLK), BF),
        in_specs=smem(1) + vmem(2),
        out_specs=vmem(1)[0],
        compiler_params=limit(4),
        name="attend",
    )(src, got, my_maps)
    attn = pair(trade(attn, PLANE))
    mixed = pl.pallas_call(
        output,
        out_shape=jax.ShapeDtypeStruct((w_out.shape[1], BLK), BF),
        in_specs=vmem(2),
        out_specs=vmem(1)[0],
        compiler_params=limit(4),
        name="output",
    )(attn, w_out.T)
    return mixed.T


def solution(mesh):
    in_specs = (
        P("frame", "chan"),
        P(None, "chan"),
        P(None, "chan"),
        P(None, "frame", None, None, None),
        P(),
    )
    return jax.shard_map(body, mesh=mesh, in_specs=in_specs, out_specs=P("frame", "chan"), check_vma=False)
```

```python
import functools

import jax
import jax.numpy as jnp
from jax import lax
from jax.experimental import pallas as pl
from jax.experimental.pallas import tpu as pltpu
from jax.sharding import PartitionSpec as P

BLK = 128
SIDE = 4
CORES = 2
BF = jnp.bfloat16
F32 = jnp.float32
R4 = range(SIDE)
STEPS = (0, 1, 3, 2)


def at(x, y, core):
    return ((x % SIDE) * SIDE + y % SIDE) * CORES + core


ALL = [(x, y, c) for x in R4 for y in R4 for c in range(CORES)]
CROSS = [[at(x, y, 0) for x in R4] for y in R4] + [[at(x, y, 1) for y in R4] for x in R4]
PLANE = [[at(x, y, c) for x in R4 for y in R4] for c in range(CORES)]
PAIRS = [[at(x, y, c) for c in range(CORES)] for x in R4 for y in R4]


def along(k):
    return [(at(x, y, c), at(x, y + k, c) if c == 0 else at(x + k, y, c)) for x, y, c in ALL]


def here_at():
    chan = lax.axis_index("chan")
    head, core = lax.div(chan, CORES), lax.rem(chan, CORES)
    return core, jnp.where(core == 0, lax.rem(head, SIDE), lax.div(head, SIDE)), head


def halve(both, out):
    size = out.shape[1]
    core = here_at()[0]
    for c in range(CORES):

        @pl.when(core == c)
        def _(start=c * (both.shape[2] - size)):
            out[...] = jnp.concatenate([both[i, :, start : start + size] for i in range(CORES)], axis=0)


def pack(w, out):
    span = w.shape[2] // SIDE
    piece = span // SIDE
    cols = jnp.concatenate([w[0], w[1]], axis=0)
    core = here_at()[0]

    @pl.when(core == 0)
    def _():
        for a in R4:
            out[a] = cols[:, a * span : (a + 1) * span]

    @pl.when(core == 1)
    def _():
        for a in R4:
            starts = [(b * SIDE + a) * piece for b in R4]
            out[a] = jnp.concatenate([cols[:, s : s + piece] for s in starts], axis=1)


def prepare(blocks_dev, lists, maps, idx, src, mine, sem):
    head, frame = here_at()[2], lax.axis_index("frame")
    copy = pltpu.make_async_copy(maps.at[head, 0], mine, sem)
    copy.start()
    for q in range(idx.shape[0]):
        place = jnp.int32(0)
        for s in range(lists.shape[1]):
            local = lists[head, s, q] - frame * blocks_dev
            place = jnp.where((local >= 0) & (local < blocks_dev), local, place)
        idx[q] = place
    for s in range(lists.shape[1]):
        src[s] = lax.div(lists[head, s, frame], jnp.int32(blocks_dev))
    copy.wait()


def project(idx, wall, *rest):
    chunks, (out, gath) = rest[:-2], rest[-2:]
    b = here_at()[1]
    for k, chunk in zip(STEPS, chunks):
        rows = chunk.shape[0]
        start = pl.multiple_of(lax.rem(b + SIDE - k, SIDE) * rows, rows)
        gath[pl.ds(start, rows), :] = chunk[...]
    w = wall[...].reshape(-1, wall.shape[2])
    out[...] = jnp.dot(w, gath[...], preferred_element_type=F32).astype(BF).reshape(out.shape)


def fold(blocks_dev, idx_from, part, own, oth, vals, idx, sem):
    fetch = pltpu.make_async_copy(idx_from, idx, sem)
    fetch.start()
    total = part[0].astype(F32)
    for a in R4[1:]:
        total += part[a].astype(F32)
    vals[...] = total.astype(BF)
    fetch.wait()
    core = here_at()[0]
    width = own.shape[1]
    half = vals.shape[1] // BLK
    mine = pl.ds(pl.multiple_of(core * width, width), width)
    theirs = pl.ds(pl.multiple_of((1 - core) * width, width), width)
    for q in range(own.shape[0]):
        here = (idx[q] < half) == (core == 0)
        block = jnp.clip(idx[q] - core * (blocks_dev - half), 0, half - 1)
        at_q = pl.ds(pl.multiple_of(block * BLK, BLK), BLK)
        own[q] = jnp.where(here, vals[mine, at_q], jnp.zeros((), BF))
        oth[q] = jnp.where(here, vals[theirs, at_q], jnp.zeros((), BF))


def merge(own, pair, out):
    out[...] = own[...] + pair[1 - here_at()[0]]


def attend(src, got, maps, out):
    acc = jnp.zeros(out.shape[1:], F32)
    for s in range(maps.shape[0]):
        acc += lax.dot_general(
            got[src[s]], maps[s], (((1,), (1,)), ((), ())), preferred_element_type=F32
        )
    acc = acc.astype(BF)
    for k in range(out.shape[0]):
        out[k] = acc


def output(attn, w, out):
    rows = [attn[c, chip] for chip in range(attn.shape[1]) for c in range(CORES)]
    out[...] = jnp.dot(w[...], jnp.concatenate(rows, axis=0), preferred_element_type=F32).astype(BF)


def hold(xs):
    whole = [pl.BlockSpec(memory_space=pl.ANY)] * len(xs)
    return pl.pallas_call(
        lambda *refs: None,
        out_shape=[jax.ShapeDtypeStruct(x.shape, x.dtype) for x in xs],
        in_specs=whole,
        out_specs=whole,
        input_output_aliases={i: i for i in range(len(xs))},
        cost_estimate=pl.CostEstimate(flops=2 * 10**10, bytes_accessed=10**7, transcendentals=0),
        compiler_params=limit(1),
        name="hold",
    )(*xs)


def vmem(n):
    return [pl.BlockSpec(memory_space=pltpu.VMEM)] * n


def smem(n):
    return [pl.BlockSpec(memory_space=pltpu.SMEM)] * n


def limit(mib):
    return pltpu.CompilerParams(vmem_limit_bytes=mib * 2**20)


def body(features, w_value, w_out, maps, lists):
    kv_rows, feat = features.shape
    width = w_value.shape[1]
    def send(v, perm):
        return lax.ppermute(v, "chan", perm)

    def trade(v, groups):
        return lax.all_to_all(v, "chan", 0, 0, axis_index_groups=groups, tiled=True)

    def pair(v):
        return lax.all_gather(v, "chan", axis_index_groups=PAIRS)

    blocks_dev = kv_rows // BLK
    half = (blocks_dev + 1) // CORES
    both = pl.pallas_call(
        halve,
        out_shape=jax.ShapeDtypeStruct((CORES * feat, half * BLK), BF),
        in_specs=vmem(1),
        out_specs=vmem(1)[0],
        compiler_params=limit(4),
        name="halve",
    )(pair(features.T))
    chunks = [both, *hold([send(both, along(k)) for k in STEPS[1:]])]
    wall = pl.pallas_call(
        pack,
        out_shape=jax.ShapeDtypeStruct((SIDE, CORES * width, SIDE * CORES * feat), BF),
        in_specs=vmem(1),
        out_specs=vmem(1)[0],
        compiler_params=limit(4),
        name="pack",
    )(pair(w_value.T))
    wall = trade(wall, CROSS)

    queries, slots = lists.shape[1:]
    idx, src, my_maps = pl.pallas_call(
        functools.partial(prepare, blocks_dev),
        out_shape=(
            jax.ShapeDtypeStruct((queries,), jnp.int32),
            jax.ShapeDtypeStruct((slots,), jnp.int32),
            jax.ShapeDtypeStruct((slots, BLK, BLK), BF),
        ),
        in_specs=smem(1) + [pl.BlockSpec(memory_space=pltpu.HBM)],
        out_specs=smem(2) + vmem(1),
        scratch_shapes=[pltpu.SemaphoreType.DMA],
        compiler_params=limit(4),
        name="prepare",
    )(lists.transpose(0, 2, 1), maps)

    part = pl.pallas_call(
        project,
        out_shape=jax.ShapeDtypeStruct((SIDE, CORES * width, half * BLK), BF),
        in_specs=[pl.BlockSpec(memory_space=pl.ANY)] + vmem(5),
        out_specs=vmem(1)[0],
        scratch_shapes=[pltpu.VMEM((SIDE * CORES * feat, half * BLK), BF)],
        compiler_params=limit(20),
        name="project",
    )(idx, wall, *chunks)
    part = trade(part, CROSS)
    side = jax.ShapeDtypeStruct((queries, width, BLK), BF)
    own, oth = pl.pallas_call(
        functools.partial(fold, blocks_dev),
        out_shape=(side, side),
        in_specs=[pl.BlockSpec(memory_space=pl.ANY)] + vmem(1),
        out_specs=vmem(2),
        scratch_shapes=[
            pltpu.VMEM((CORES * width, half * BLK), BF),
            pltpu.SMEM((queries,), jnp.int32),
            pltpu.SemaphoreType.DMA,
        ],
        compiler_params=limit(8),
        name="fold",
    )(idx, part)
    blocks = pl.pallas_call(
        merge,
        out_shape=side,
        in_specs=vmem(2),
        out_specs=vmem(1)[0],
        compiler_params=limit(4),
        name="merge",
    )(own, pair(oth))
    got = lax.all_to_all(blocks, "frame", 0, 0, tiled=True)
    attn = pl.pallas_call(
        attend,
        out_shape=jax.ShapeDtypeStruct((SIDE * SIDE, width, BLK), BF),
        in_specs=smem(1) + vmem(2),
        out_specs=vmem(1)[0],
        compiler_params=limit(4),
        name="attend",
    )(src, got, my_maps)
    attn = pair(trade(attn, PLANE))
    mixed = pl.pallas_call(
        output,
        out_shape=jax.ShapeDtypeStruct((w_out.shape[1], BLK), BF),
        in_specs=vmem(2),
        out_specs=vmem(1)[0],
        compiler_params=limit(4),
        name="output",
    )(attn, w_out.T)
    return mixed.T


def solution(mesh):
    in_specs = (
        P("frame", "chan"),
        P(None, "chan"),
        P(None, "chan"),
        P(None, "frame", None, None, None),
        P(),
    )
    return jax.shard_map(body, mesh=mesh, in_specs=in_specs, out_specs=P("frame", "chan"), check_vma=False)
```

```python
import functools

import jax
import jax.numpy as jnp
from jax import lax
from jax.experimental import pallas as pl
from jax.experimental.pallas import tpu as pltpu
from jax.sharding import PartitionSpec as P

BLK = 128
SIDE = 4
CORES = 2
BF = jnp.bfloat16
F32 = jnp.float32
R4 = range(SIDE)
STEPS = (0, 1, 3, 2)


def at(x, y, core):
    return ((x % SIDE) * SIDE + y % SIDE) * CORES + core


ALL = [(x, y, c) for x in R4 for y in R4 for c in range(CORES)]
CROSS = [[at(x, y, 0) for x in R4] for y in R4] + [[at(x, y, 1) for y in R4] for x in R4]
PLANE = [[at(x, y, c) for x in R4 for y in R4] for c in range(CORES)]
PAIRS = [[at(x, y, c) for c in range(CORES)] for x in R4 for y in R4]


def along(k):
    return [(at(x, y, c), at(x, y + k, c) if c == 0 else at(x + k, y, c)) for x, y, c in ALL]


def here_at():
    chan = lax.axis_index("chan")
    head, core = lax.div(chan, CORES), lax.rem(chan, CORES)
    return core, jnp.where(core == 0, lax.rem(head, SIDE), lax.div(head, SIDE)), head


def halve(both, out):
    size = out.shape[1]
    core = here_at()[0]
    for c in range(CORES):

        @pl.when(core == c)
        def _(start=c * (both.shape[2] - size)):
            out[...] = jnp.concatenate([both[i, :, start : start + size] for i in range(CORES)], axis=0)


def pack(w, out):
    span = w.shape[2] // SIDE
    piece = span // SIDE
    cols = jnp.concatenate([w[0], w[1]], axis=0)
    core = here_at()[0]

    @pl.when(core == 0)
    def _():
        for a in R4:
            out[a] = cols[:, a * span : (a + 1) * span]

    @pl.when(core == 1)
    def _():
        for a in R4:
            starts = [(b * SIDE + a) * piece for b in R4]
            out[a] = jnp.concatenate([cols[:, s : s + piece] for s in starts], axis=1)


def prepare(blocks_dev, lists, maps, idx, src, mine, sem):
    head, frame = here_at()[2], lax.axis_index("frame")
    copy = pltpu.make_async_copy(maps.at[head, 0], mine, sem)
    copy.start()
    for q in range(idx.shape[0]):
        place = jnp.int32(0)
        for s in range(lists.shape[1]):
            local = lists[head, s, q] - frame * blocks_dev
            place = jnp.where((local >= 0) & (local < blocks_dev), local, place)
        idx[q] = place
    for s in range(lists.shape[1]):
        src[s] = lax.div(lists[head, s, frame], jnp.int32(blocks_dev))
    copy.wait()


def assemble(*refs):
    chunks, gath = refs[:-1], refs[-1]
    b = here_at()[1]
    for k, chunk in zip(STEPS, chunks):
        rows = chunk.shape[0]
        start = pl.multiple_of(lax.rem(b + SIDE - k, SIDE) * rows, rows)
        gath[pl.ds(start, rows), :] = chunk[...]


def project(idx, wall, gath, out):
    w = wall[...].reshape(-1, wall.shape[2])
    out[...] = jnp.dot(w, gath[...], preferred_element_type=F32).astype(BF).reshape(out.shape)


def fold(blocks_dev, idx_from, part, own, oth, vals, idx, sem):
    fetch = pltpu.make_async_copy(idx_from, idx, sem)
    fetch.start()
    total = part[0].astype(F32)
    for a in R4[1:]:
        total += part[a].astype(F32)
    vals[...] = total.astype(BF)
    fetch.wait()
    core = here_at()[0]
    width = own.shape[1]
    half = vals.shape[1] // BLK
    mine = pl.ds(pl.multiple_of(core * width, width), width)
    theirs = pl.ds(pl.multiple_of((1 - core) * width, width), width)
    for q in range(own.shape[0]):
        here = (idx[q] < half) == (core == 0)
        block = jnp.clip(idx[q] - core * (blocks_dev - half), 0, half - 1)
        at_q = pl.ds(pl.multiple_of(block * BLK, BLK), BLK)
        own[q] = jnp.where(here, vals[mine, at_q], jnp.zeros((), BF))
        oth[q] = jnp.where(here, vals[theirs, at_q], jnp.zeros((), BF))


def merge(own, pair, out):
    out[...] = own[...] + pair[1 - here_at()[0]]


def attend(src, got, maps, out):
    acc = jnp.zeros(out.shape[1:], F32)
    for s in range(maps.shape[0]):
        acc += lax.dot_general(
            got[src[s]], maps[s], (((1,), (1,)), ((), ())), preferred_element_type=F32
        )
    acc = acc.astype(BF)
    for k in range(out.shape[0]):
        out[k] = acc


def output(attn, w, out):
    rows = [attn[c, chip] for chip in range(attn.shape[1]) for c in range(CORES)]
    out[...] = jnp.dot(w[...], jnp.concatenate(rows, axis=0), preferred_element_type=F32).astype(BF)


def vmem(n):
    return [pl.BlockSpec(memory_space=pltpu.VMEM)] * n


def smem(n):
    return [pl.BlockSpec(memory_space=pltpu.SMEM)] * n


def limit(mib):
    return pltpu.CompilerParams(vmem_limit_bytes=mib * 2**20)


def body(features, w_value, w_out, maps, lists):
    kv_rows, feat = features.shape
    width = w_value.shape[1]
    def send(v, perm):
        return lax.ppermute(v, "chan", perm)

    def trade(v, groups):
        return lax.all_to_all(v, "chan", 0, 0, axis_index_groups=groups, tiled=True)

    def pair(v):
        return lax.all_gather(v, "chan", axis_index_groups=PAIRS)

    blocks_dev = kv_rows // BLK
    half = (blocks_dev + 1) // CORES
    both = pl.pallas_call(
        halve,
        out_shape=jax.ShapeDtypeStruct((CORES * feat, half * BLK), BF),
        in_specs=vmem(1),
        out_specs=vmem(1)[0],
        compiler_params=limit(4),
        name="halve",
    )(pair(features.T))
    chunks = [both] + [send(both, along(k)) for k in STEPS[1:]]
    gath = pl.pallas_call(
        assemble,
        out_shape=jax.ShapeDtypeStruct((SIDE * CORES * feat, half * BLK), BF),
        in_specs=vmem(SIDE),
        out_specs=vmem(1)[0],
        cost_estimate=pl.CostEstimate(flops=2 * 10**10, bytes_accessed=10**7, transcendentals=0),
        compiler_params=limit(8),
        name="assemble",
    )(*chunks)

    wall = pl.pallas_call(
        pack,
        out_shape=jax.ShapeDtypeStruct((SIDE, CORES * width, SIDE * CORES * feat), BF),
        in_specs=vmem(1),
        out_specs=vmem(1)[0],
        compiler_params=limit(4),
        name="pack",
    )(pair(w_value.T))
    wall = trade(wall, CROSS)

    queries, slots = lists.shape[1:]
    idx, src, my_maps = pl.pallas_call(
        functools.partial(prepare, blocks_dev),
        out_shape=(
            jax.ShapeDtypeStruct((queries,), jnp.int32),
            jax.ShapeDtypeStruct((slots,), jnp.int32),
            jax.ShapeDtypeStruct((slots, BLK, BLK), BF),
        ),
        in_specs=smem(1) + [pl.BlockSpec(memory_space=pltpu.HBM)],
        out_specs=smem(2) + vmem(1),
        scratch_shapes=[pltpu.SemaphoreType.DMA],
        compiler_params=limit(4),
        name="prepare",
    )(lists.transpose(0, 2, 1), maps)

    part = pl.pallas_call(
        project,
        out_shape=jax.ShapeDtypeStruct((SIDE, CORES * width, half * BLK), BF),
        in_specs=[pl.BlockSpec(memory_space=pl.ANY)] + vmem(2),
        out_specs=vmem(1)[0],
        compiler_params=limit(16),
        name="project",
    )(idx, wall, gath)
    part = trade(part, CROSS)
    side = jax.ShapeDtypeStruct((queries, width, BLK), BF)
    own, oth = pl.pallas_call(
        functools.partial(fold, blocks_dev),
        out_shape=(side, side),
        in_specs=[pl.BlockSpec(memory_space=pl.ANY)] + vmem(1),
        out_specs=vmem(2),
        scratch_shapes=[
            pltpu.VMEM((CORES * width, half * BLK), BF),
            pltpu.SMEM((queries,), jnp.int32),
            pltpu.SemaphoreType.DMA,
        ],
        compiler_params=limit(8),
        name="fold",
    )(idx, part)
    blocks = pl.pallas_call(
        merge,
        out_shape=side,
        in_specs=vmem(2),
        out_specs=vmem(1)[0],
        compiler_params=limit(4),
        name="merge",
    )(own, pair(oth))
    got = lax.all_to_all(blocks, "frame", 0, 0, tiled=True)
    attn = pl.pallas_call(
        attend,
        out_shape=jax.ShapeDtypeStruct((SIDE * SIDE, width, BLK), BF),
        in_specs=smem(1) + vmem(2),
        out_specs=vmem(1)[0],
        compiler_params=limit(4),
        name="attend",
    )(src, got, my_maps)
    attn = pair(trade(attn, PLANE))
    mixed = pl.pallas_call(
        output,
        out_shape=jax.ShapeDtypeStruct((w_out.shape[1], BLK), BF),
        in_specs=vmem(2),
        out_specs=vmem(1)[0],
        compiler_params=limit(4),
        name="output",
    )(attn, w_out.T)
    return mixed.T


def solution(mesh):
    in_specs = (
        P("frame", "chan"),
        P(None, "chan"),
        P(None, "chan"),
        P(None, "frame", None, None, None),
        P(),
    )
    return jax.shard_map(body, mesh=mesh, in_specs=in_specs, out_specs=P("frame", "chan"), check_vma=False)
```

```python
import functools

import jax
import jax.numpy as jnp
from jax import lax
from jax.experimental import pallas as pl
from jax.experimental.pallas import tpu as pltpu
from jax.sharding import PartitionSpec as P

BLK = 128
SIDE = 4
CORES = 2
BF = jnp.bfloat16
F32 = jnp.float32
R4 = range(SIDE)
STEPS = (0, 2, 3, 1)


def at(x, y, core):
    return ((x % SIDE) * SIDE + y % SIDE) * CORES + core


ALL = [(x, y, c) for x in R4 for y in R4 for c in range(CORES)]
CROSS = [[at(x, y, 0) for x in R4] for y in R4] + [[at(x, y, 1) for y in R4] for x in R4]
PLANE = [[at(x, y, c) for x in R4 for y in R4] for c in range(CORES)]
PAIRS = [[at(x, y, c) for c in range(CORES)] for x in R4 for y in R4]


def along(k):
    return [(at(x, y, c), at(x, y + k, c) if c == 0 else at(x + k, y, c)) for x, y, c in ALL]


def here_at():
    chan = lax.axis_index("chan")
    head, core = lax.div(chan, CORES), lax.rem(chan, CORES)
    return core, jnp.where(core == 0, lax.rem(head, SIDE), lax.div(head, SIDE)), head


def pack(w, out):
    feat = w.shape[2] // (SIDE * SIDE * CORES)
    cols = jnp.concatenate([w[0], w[1]], axis=0)
    core = here_at()[0]
    for c in range(CORES):

        @pl.when(core == c)
        def _(c=c):
            for a in R4:
                chips = [a * SIDE + b if c == 0 else b * SIDE + a for b in R4]
                starts = [(chip * CORES + c) * feat for chip in chips]
                out[a] = jnp.concatenate([cols[:, s : s + feat] for s in starts], axis=1)


def prepare(blocks_dev, lists, maps, idx, src, mine, sem):
    core, b, head = here_at()
    frame = lax.axis_index("frame")
    copy = pltpu.make_async_copy(maps.at[head, 0], mine, sem)
    copy.start()
    for a in R4:
        partner = jnp.where(core == 0, a * SIDE + b, b * SIDE + a)
        for q in range(idx.shape[1]):
            place = jnp.int32(0)
            for s in range(lists.shape[1]):
                local = lists[partner, s, q] - frame * blocks_dev
                place = jnp.where((local >= 0) & (local < blocks_dev), local, place)
            idx[a, q] = place
    for s in range(lists.shape[1]):
        src[s] = lax.div(lists[head, s, frame], jnp.int32(blocks_dev))
    copy.wait()


def assemble(*refs):
    chunks, gath = refs[:-1], refs[-1]
    b = here_at()[1]
    for k, chunk in zip(STEPS, chunks):
        rows = chunk.shape[0]
        start = pl.multiple_of(lax.rem(b + SIDE - k, SIDE) * rows, rows)
        gath[pl.ds(start, rows), :] = chunk[...]


def project(idx_from, wall, gath, out, vals, idx, sem):
    fetch = pltpu.make_async_copy(idx_from, idx, sem)
    fetch.start()
    vals[...] = jnp.dot(wall[...].reshape(-1, wall.shape[2]), gath[...], preferred_element_type=F32).astype(BF)
    fetch.wait()
    rows = out.shape[2]
    for a in R4:
        for q in range(out.shape[1]):
            start = pl.multiple_of(idx[a, q] * BLK, BLK)
            out[a, q] = vals[a * rows : (a + 1) * rows, pl.ds(start, BLK)]


def fold(part, own, oth):
    width = own.shape[1]
    core = here_at()[0]
    for c in range(CORES):

        @pl.when(core == c)
        def _(c=c):
            for q in range(own.shape[0]):
                total = part[0, q].astype(F32)
                for a in R4[1:]:
                    total += part[a, q].astype(F32)
                own[q] = total[c * width : (c + 1) * width]
                oth[q] = total[(1 - c) * width : (2 - c) * width].astype(BF)


def merge(own, pair, out):
    out[...] = (own[...] + pair[1 - here_at()[0]].astype(F32)).astype(BF)


def attend(src, got, maps, out):
    acc = jnp.zeros(out.shape[1:], F32)
    for s in range(maps.shape[0]):
        acc += lax.dot_general(
            got[src[s]], maps[s], (((1,), (1,)), ((), ())), preferred_element_type=F32
        )
    acc = acc.astype(BF)
    for k in range(out.shape[0]):
        out[k] = acc


def output(attn, w, out):
    rows = [attn[c, chip] for chip in range(attn.shape[1]) for c in range(CORES)]
    out[...] = jnp.dot(w[...], jnp.concatenate(rows, axis=0), preferred_element_type=F32).astype(BF)


def vmem(n):
    return [pl.BlockSpec(memory_space=pltpu.VMEM)] * n


def smem(n):
    return [pl.BlockSpec(memory_space=pltpu.SMEM)] * n


def limit(mib):
    return pltpu.CompilerParams(vmem_limit_bytes=mib * 2**20)


def body(features, w_value, w_out, maps, lists):
    kv_rows, feat = features.shape
    width = w_value.shape[1]
    def send(v, perm):
        return lax.ppermute(v, "chan", perm)

    def trade(v, groups):
        return lax.all_to_all(v, "chan", 0, 0, axis_index_groups=groups, tiled=True)

    def pair(v):
        return lax.all_gather(v, "chan", axis_index_groups=PAIRS)

    blocks_dev = kv_rows // BLK
    ft = features.T
    chunks = [ft] + [send(ft, along(k)) for k in STEPS[1:]]
    gath = pl.pallas_call(
        assemble,
        out_shape=jax.ShapeDtypeStruct((SIDE * feat, kv_rows), BF),
        in_specs=vmem(SIDE),
        out_specs=vmem(1)[0],
        cost_estimate=pl.CostEstimate(flops=2 * 10**10, bytes_accessed=10**7, transcendentals=0),
        compiler_params=limit(8),
        name="assemble",
    )(*chunks)

    wall = pl.pallas_call(
        pack,
        out_shape=jax.ShapeDtypeStruct((SIDE, CORES * width, SIDE * feat), BF),
        in_specs=vmem(1),
        out_specs=vmem(1)[0],
        compiler_params=limit(4),
        name="pack",
    )(pair(w_value.T))
    wall = trade(wall, CROSS)

    queries, slots = lists.shape[1:]
    idx, src, my_maps = pl.pallas_call(
        functools.partial(prepare, blocks_dev),
        out_shape=(
            jax.ShapeDtypeStruct((SIDE, queries), jnp.int32),
            jax.ShapeDtypeStruct((slots,), jnp.int32),
            jax.ShapeDtypeStruct((slots, BLK, BLK), BF),
        ),
        in_specs=smem(1) + [pl.BlockSpec(memory_space=pltpu.HBM)],
        out_specs=smem(2) + vmem(1),
        scratch_shapes=[pltpu.SemaphoreType.DMA],
        compiler_params=limit(4),
        name="prepare",
    )(lists.transpose(0, 2, 1), maps)

    part = pl.pallas_call(
        project,
        out_shape=jax.ShapeDtypeStruct((SIDE, queries, CORES * width, BLK), BF),
        in_specs=[pl.BlockSpec(memory_space=pl.ANY)] + vmem(2),
        out_specs=vmem(1)[0],
        scratch_shapes=[
            pltpu.VMEM((SIDE * CORES * width, kv_rows), BF),
            pltpu.SMEM((SIDE, queries), jnp.int32),
            pltpu.SemaphoreType.DMA,
        ],
        compiler_params=limit(20),
        name="project",
    )(idx, wall, gath)
    part = trade(part, CROSS)
    side = jax.ShapeDtypeStruct((queries, width, BLK), BF)
    own, oth = pl.pallas_call(
        fold,
        out_shape=(jax.ShapeDtypeStruct(side.shape, F32), side),
        in_specs=vmem(1),
        out_specs=vmem(2),
        compiler_params=limit(8),
        name="fold",
    )(part)
    blocks = pl.pallas_call(
        merge,
        out_shape=side,
        in_specs=vmem(2),
        out_specs=vmem(1)[0],
        compiler_params=limit(4),
        name="merge",
    )(own, pair(oth))
    got = lax.all_to_all(blocks, "frame", 0, 0, tiled=True)
    attn = pl.pallas_call(
        attend,
        out_shape=jax.ShapeDtypeStruct((SIDE * SIDE, width, BLK), BF),
        in_specs=smem(1) + vmem(2),
        out_specs=vmem(1)[0],
        compiler_params=limit(4),
        name="attend",
    )(src, got, my_maps)
    attn = pair(trade(attn, PLANE))
    mixed = pl.pallas_call(
        output,
        out_shape=jax.ShapeDtypeStruct((w_out.shape[1], BLK), BF),
        in_specs=vmem(2),
        out_specs=vmem(1)[0],
        compiler_params=limit(4),
        name="output",
    )(attn, w_out.T)
    return mixed.T


def solution(mesh):
    in_specs = (
        P("frame", "chan"),
        P(None, "chan"),
        P(None, "chan"),
        P(None, "frame", None, None, None),
        P(),
    )
    return jax.shard_map(body, mesh=mesh, in_specs=in_specs, out_specs=P("frame", "chan"), check_vma=False)
```

```python
import functools

import jax
import jax.numpy as jnp
from jax import lax
from jax.experimental import pallas as pl
from jax.experimental.pallas import tpu as pltpu
from jax.sharding import PartitionSpec as P

BLK = 128
SIDE = 4
CORES = 2
BF = jnp.bfloat16
F32 = jnp.float32
R4 = range(SIDE)
STEPS = (0, 3, 2, 1)


def at(x, y, core):
    return ((x % SIDE) * SIDE + y % SIDE) * CORES + core


ALL = [(x, y, c) for x in R4 for y in R4 for c in range(CORES)]
CROSS = [[at(x, y, 0) for x in R4] for y in R4] + [[at(x, y, 1) for y in R4] for x in R4]
PLANE = [[at(x, y, c) for x in R4 for y in R4] for c in range(CORES)]
PAIRS = [[at(x, y, c) for c in range(CORES)] for x in R4 for y in R4]


def along(k):
    return [(at(x, y, c), at(x, y + k, c) if c == 0 else at(x + k, y, c)) for x, y, c in ALL]


def here_at():
    chan = lax.axis_index("chan")
    head, core = lax.div(chan, CORES), lax.rem(chan, CORES)
    return core, jnp.where(core == 0, lax.rem(head, SIDE), lax.div(head, SIDE)), head


def pack(w, out):
    feat = w.shape[2] // (SIDE * SIDE * CORES)
    cols = jnp.concatenate([w[0], w[1]], axis=0)
    core = here_at()[0]
    for c in range(CORES):

        @pl.when(core == c)
        def _(c=c):
            for a in R4:
                chips = [a * SIDE + b if c == 0 else b * SIDE + a for b in R4]
                starts = [(chip * CORES + c) * feat for chip in chips]
                out[a] = jnp.concatenate([cols[:, s : s + feat] for s in starts], axis=1)


def prepare(blocks_dev, lists, maps, idx, src, mine, sem):
    core, b, head = here_at()
    frame = lax.axis_index("frame")
    copy = pltpu.make_async_copy(maps.at[head, 0], mine, sem)
    copy.start()
    for a in R4:
        partner = jnp.where(core == 0, a * SIDE + b, b * SIDE + a)
        for q in range(idx.shape[1]):
            place = jnp.int32(0)
            for s in range(lists.shape[1]):
                local = lists[partner, s, q] - frame * blocks_dev
                place = jnp.where((local >= 0) & (local < blocks_dev), local, place)
            idx[a, q] = place
    for s in range(lists.shape[1]):
        src[s] = lax.div(lists[head, s, frame], jnp.int32(blocks_dev))
    copy.wait()


def assemble(*refs):
    chunks, gath = refs[:-1], refs[-1]
    b = here_at()[1]
    for k, chunk in zip(STEPS, chunks):
        rows = chunk.shape[0]
        start = pl.multiple_of(lax.rem(b + SIDE - k, SIDE) * rows, rows)
        gath[pl.ds(start, rows), :] = chunk[...]


def project(idx_from, wall, gath, out, vals, idx, sem):
    fetch = pltpu.make_async_copy(idx_from, idx, sem)
    fetch.start()
    vals[...] = jnp.dot(wall[...].reshape(-1, wall.shape[2]), gath[...], preferred_element_type=F32).astype(BF)
    fetch.wait()
    rows = out.shape[2]
    for a in R4:
        for q in range(out.shape[1]):
            start = pl.multiple_of(idx[a, q] * BLK, BLK)
            out[a, q] = vals[a * rows : (a + 1) * rows, pl.ds(start, BLK)]


def fold(part, own, oth):
    width = own.shape[1]
    core = here_at()[0]
    for c in range(CORES):

        @pl.when(core == c)
        def _(c=c):
            for q in range(own.shape[0]):
                total = part[0, q].astype(F32)
                for a in R4[1:]:
                    total += part[a, q].astype(F32)
                own[q] = total[c * width : (c + 1) * width]
                oth[q] = total[(1 - c) * width : (2 - c) * width].astype(BF)


def merge(own, pair, out):
    out[...] = (own[...] + pair[1 - here_at()[0]].astype(F32)).astype(BF)


def attend(src, got, maps, out):
    acc = jnp.zeros(out.shape[1:], F32)
    for s in range(maps.shape[0]):
        acc += lax.dot_general(
            got[src[s]], maps[s], (((1,), (1,)), ((), ())), preferred_element_type=F32
        )
    acc = acc.astype(BF)
    for k in range(out.shape[0]):
        out[k] = acc


def output(attn, w, out):
    rows = [attn[c, chip] for chip in range(attn.shape[1]) for c in range(CORES)]
    out[...] = jnp.dot(w[...], jnp.concatenate(rows, axis=0), preferred_element_type=F32).astype(BF)


def vmem(n):
    return [pl.BlockSpec(memory_space=pltpu.VMEM)] * n


def smem(n):
    return [pl.BlockSpec(memory_space=pltpu.SMEM)] * n


def limit(mib):
    return pltpu.CompilerParams(vmem_limit_bytes=mib * 2**20)


def body(features, w_value, w_out, maps, lists):
    kv_rows, feat = features.shape
    width = w_value.shape[1]
    def send(v, perm):
        return lax.ppermute(v, "chan", perm)

    def trade(v, groups):
        return lax.all_to_all(v, "chan", 0, 0, axis_index_groups=groups, tiled=True)

    def pair(v):
        return lax.all_gather(v, "chan", axis_index_groups=PAIRS)

    blocks_dev = kv_rows // BLK
    ft = features.T
    chunks = [ft] + [send(ft, along(k)) for k in STEPS[1:]]
    gath = pl.pallas_call(
        assemble,
        out_shape=jax.ShapeDtypeStruct((SIDE * feat, kv_rows), BF),
        in_specs=vmem(SIDE),
        out_specs=vmem(1)[0],
        cost_estimate=pl.CostEstimate(flops=2 * 10**10, bytes_accessed=10**7, transcendentals=0),
        compiler_params=limit(8),
        name="assemble",
    )(*chunks)

    wall = pl.pallas_call(
        pack,
        out_shape=jax.ShapeDtypeStruct((SIDE, CORES * width, SIDE * feat), BF),
        in_specs=vmem(1),
        out_specs=vmem(1)[0],
        compiler_params=limit(4),
        name="pack",
    )(pair(w_value.T))
    wall = trade(wall, CROSS)

    queries, slots = lists.shape[1:]
    idx, src, my_maps = pl.pallas_call(
        functools.partial(prepare, blocks_dev),
        out_shape=(
            jax.ShapeDtypeStruct((SIDE, queries), jnp.int32),
            jax.ShapeDtypeStruct((slots,), jnp.int32),
            jax.ShapeDtypeStruct((slots, BLK, BLK), BF),
        ),
        in_specs=smem(1) + [pl.BlockSpec(memory_space=pltpu.HBM)],
        out_specs=smem(2) + vmem(1),
        scratch_shapes=[pltpu.SemaphoreType.DMA],
        compiler_params=limit(4),
        name="prepare",
    )(lists.transpose(0, 2, 1), maps)

    part = pl.pallas_call(
        project,
        out_shape=jax.ShapeDtypeStruct((SIDE, queries, CORES * width, BLK), BF),
        in_specs=[pl.BlockSpec(memory_space=pl.ANY)] + vmem(2),
        out_specs=vmem(1)[0],
        scratch_shapes=[
            pltpu.VMEM((SIDE * CORES * width, kv_rows), BF),
            pltpu.SMEM((SIDE, queries), jnp.int32),
            pltpu.SemaphoreType.DMA,
        ],
        compiler_params=limit(20),
        name="project",
    )(idx, wall, gath)
    part = trade(part, CROSS)
    side = jax.ShapeDtypeStruct((queries, width, BLK), BF)
    own, oth = pl.pallas_call(
        fold,
        out_shape=(jax.ShapeDtypeStruct(side.shape, F32), side),
        in_specs=vmem(1),
        out_specs=vmem(2),
        compiler_params=limit(8),
        name="fold",
    )(part)
    blocks = pl.pallas_call(
        merge,
        out_shape=side,
        in_specs=vmem(2),
        out_specs=vmem(1)[0],
        compiler_params=limit(4),
        name="merge",
    )(own, pair(oth))
    got = lax.all_to_all(blocks, "frame", 0, 0, tiled=True)
    attn = pl.pallas_call(
        attend,
        out_shape=jax.ShapeDtypeStruct((SIDE * SIDE, width, BLK), BF),
        in_specs=smem(1) + vmem(2),
        out_specs=vmem(1)[0],
        compiler_params=limit(4),
        name="attend",
    )(src, got, my_maps)
    attn = pair(trade(attn, PLANE))
    mixed = pl.pallas_call(
        output,
        out_shape=jax.ShapeDtypeStruct((w_out.shape[1], BLK), BF),
        in_specs=vmem(2),
        out_specs=vmem(1)[0],
        compiler_params=limit(4),
        name="output",
    )(attn, w_out.T)
    return mixed.T


def solution(mesh):
    in_specs = (
        P("frame", "chan"),
        P(None, "chan"),
        P(None, "chan"),
        P(None, "frame", None, None, None),
        P(),
    )
    return jax.shard_map(body, mesh=mesh, in_specs=in_specs, out_specs=P("frame", "chan"), check_vma=False)
```
